32 devices in a mesh: virt: 8 (over y, x, core), pair: 4 (over z).
Axes of the slice: x: 2, y: 2, z: 4, core: 2. Of those that a mesh axis runs over, the one named last changes fastest.
Arguments:
- amplitudes: float32 [1024, 15360], P('pair', 'virt'), may hold values from -6 to 6
- integrals: float32 [15360, 384], P('virt'), may hold values from -0.125 to 0.125
- tile_mask: int32 [160, 4], P('virt'), may hold values from 0 to 1
- mirror_row: int32 [1024], P('pair'), may hold values from 0 to 255, as said below
Outputs:
- residual: float32 [1024, 384], P('pair', 'virt')
The draws below stay inside these ranges and needn't reach their ends.
Inputs may be any that keep to these rules, and one draw needn't show every extreme that they name: For the row at local index l on pair index q, mirror_row is the local index of its mirror pair's row on pair index (q + G / 2) mod G, G = 4; the rows of one device map one to one onto the rows of that device, and the mirror of the mirror is the row itself.
All inputs are finite; a program needn't handle non-finite values.
Results may differ from the reference program's by a relative error of at most 0.000092.
Values sent between devices are 32-bit elements; how exact they have to be, the bound alone decides.
No kernel may reach another device: no remote copies, remote signals or barrier semaphores. Data moves between devices by JAX's collectives and lax.ppermute only.
A program may use at most 64 MiB of HBM per device.

```python
import jax
import jax.numpy as jnp
from jax import lax

TILE = 96
KT_DEV = 20
MT = 4
P_DEV = 256
KTILES = 160
K = 15360
M = 384
PAIRS = 1024


def draw_tile_mask(key, part):
    key_live, key_entry, key_level = jax.random.split(key, 3)
    blocks = KTILES // KT_DEV
    level = jax.random.randint(key_level, (blocks, 1), 1, 5)
    live_rows = jax.random.randint(key_live, (blocks, KT_DEV), 0, 4) < level
    live_rows = live_rows.reshape(KTILES, 1).astype(jnp.int32)
    entries = jax.random.randint(key_entry, (KTILES, MT), 0, 2)
    return (live_rows * entries).astype(jnp.int32)


def draw_mirror_row(key, part):
    couples = PAIRS // P_DEV // 2
    subkeys = jax.random.split(key, couples)
    forward = jax.vmap(lambda subkey: jax.random.permutation(subkey, P_DEV))(subkeys).astype(jnp.int32)
    backward = jnp.argsort(forward, axis=1).astype(jnp.int32)
    return jnp.concatenate([forward, backward], axis=0).reshape(PAIRS).astype(jnp.int32)


def spiked(values, stream_key, source, target, parts, factor):
    def block_of(position):
        return (jnp.arange(values.shape[position]) // (values.shape[position] // parts)).reshape((-1,) + (1,) * (values.ndim - 1 - position))

    one_side = jax.random.permutation(stream_key, parts)[block_of(target)]
    far = (block_of(target) + parts // 2) % parts
    return jnp.where((block_of(source) == one_side) | (block_of(source) == far), factor * values, values)


def levels(rng, extent, cuts, smallest, high):
    def one(position, parts):
        heights = jax.random.uniform(jax.random.fold_in(jax.random.fold_in(rng, 6), position), (parts,), jnp.float32, smallest / len(cuts), high / len(cuts))
        return jnp.repeat(jnp.exp(heights), extent[position] // parts).reshape((-1,) + (1,) * (len(extent) - position - 1))

    factor_of = one(*cuts[0])
    for cut in cuts[1:]:
        factor_of = factor_of * one(*cut)
    return factor_of


def gaussian(own_key, extent, deviation, bound, pieces=(), kind=jnp.bfloat16):
    factor_of = levels(own_key, extent, pieces, -0.22, 0.18) if pieces else 1.0
    array = jax.random.normal(own_key, extent, jnp.float32) * deviation * factor_of
    return jnp.minimum(jnp.maximum(array, -bound), bound).astype(kind)


def heavy_noise(own_key, shape, deviation, most, pieces, heavy, held_as=jnp.bfloat16):
    array = deviation * jax.random.normal(own_key, shape, jnp.float32)
    if pieces:
        array = array * levels(own_key, shape, pieces, -0.22, 0.18)
    return jnp.clip(spiked(array, jax.random.fold_in(own_key, 3), *heavy), -most, most).astype(held_as)


def setup_inputs(seed: int = 0) -> dict:
    key_list = jax.random.split(jax.random.key(seed), 5)
    amplitudes = gaussian(key_list[0], (PAIRS, K), 1.0, 6.0, ((0, 4), (1, 8)), jnp.float32)
    integrals = heavy_noise(key_list[1], (K, M), (K // 4) ** -0.5, 0.125, ((0, 8),), (0, 1, 8, 2.0), jnp.float32)
    tile_mask = draw_tile_mask(jax.random.fold_in(key_list[4], 71), 0)
    mirror_row = draw_mirror_row(jax.random.fold_in(key_list[4], 71), 0)
    return {"amplitudes": amplitudes, "integrals": integrals, "tile_mask": tile_mask, "mirror_row": mirror_row}


def expand_mask(tile_mask):
    expanded = jnp.repeat(tile_mask.astype(jnp.float32), TILE, axis=0)
    return jnp.repeat(expanded, TILE, axis=1)


def reference(amplitudes, integrals, tile_mask, mirror_row):
    masked = integrals * expand_mask(tile_mask)
    ladder = jnp.dot(amplitudes, masked, precision=lax.Precision.HIGHEST, preferred_element_type=jnp.float32)
    turned = jnp.roll(ladder, M // 2, axis=1)
    device_count = PAIRS // P_DEV
    owners = jnp.arange(PAIRS, dtype=jnp.int32) // P_DEV
    partner = (owners + device_count // 2) % device_count
    mirror_global = (partner * P_DEV + mirror_row).astype(jnp.int32)
    return ladder + jnp.take(turned, mirror_global, axis=0)
```

```python
import functools

import jax
import jax.numpy as jnp
from jax import lax
from jax.experimental import pallas as pl
from jax.experimental.pallas import tpu as pltpu
from jax.sharding import PartitionSpec as P

CHUNK = 512
MIB = 1 << 20


def split(x):
    high = x.astype(jnp.bfloat16)
    low = (x - high.astype(jnp.float32)).astype(jnp.bfloat16)
    return high, low


def chunks_of(extent):
    return [(start, min(CHUNK, extent - start)) for start in range(0, extent, CHUNK)]


def ladder_kernel(parts, mask_ref, side_ref, amp_ref, int_ref, out_ref, amp, ints, sems):
    depth, cols = int_ref.shape
    rows = amp_ref.shape[0]
    spans = chunks_of(depth)
    copies = []
    for i, (start, size) in enumerate(spans):
        span = pl.ds(start, size)
        one = pltpu.make_async_copy(amp_ref.at[:, span], amp.at[:, span], sems.at[0, i])
        two = pltpu.make_async_copy(int_ref.at[span, :], ints.at[span, :], sems.at[1, i])
        one.start()
        two.start()
        copies.append((one, two))

    col_tiles, tile_rows = mask_ref.shape
    tile_r, tile_c = depth // tile_rows, cols // col_tiles
    lane = lax.broadcasted_iota(jnp.int32, (1, cols), 1)
    total = jnp.zeros((rows, cols), jnp.float32)
    for (start, size), (one, two) in zip(spans, copies):
        one.wait()
        two.wait()
        pieces = []
        at = start
        while at < start + size:
            t = at // tile_r
            end = min((t + 1) * tile_r, start + size)
            factor = jnp.full((1, cols), mask_ref[0, t].astype(jnp.float32))
            for u in range(1, col_tiles):
                factor = jnp.where(lane >= u * tile_c, mask_ref[u, t].astype(jnp.float32), factor)
            pieces.append(ints[at:end, :] * factor)
            at = end
        masked = jnp.concatenate(pieces, axis=0)
        b_high, b_low = split(masked)
        a_high, a_low = split(amp[:, start:start + size])
        dot = functools.partial(jnp.dot, preferred_element_type=jnp.float32)
        total += dot(a_high, b_high) + dot(a_high, b_low) + dot(a_low, b_high)
    turned = total.T
    block = cols // parts
    for b in range(parts):
        out_ref[(b % 2) ^ side_ref[0], b // 2] = turned[b * block:(b + 1) * block, :]


def ladder(parts, mask, side, amplitudes, integrals):
    rows, depth = amplitudes.shape
    cols = integrals.shape[1]
    count = len(chunks_of(depth))
    return pl.pallas_call(
        functools.partial(ladder_kernel, parts),
        out_shape=jax.ShapeDtypeStruct((2, parts // 2, cols // parts, rows), jnp.float32),
        in_specs=[pl.BlockSpec(memory_space=pltpu.SMEM)] * 2 + [pl.BlockSpec(memory_space=pl.ANY)] * 2,
        out_specs=pl.BlockSpec(memory_space=pltpu.VMEM),
        scratch_shapes=[
            pltpu.VMEM((rows, depth), jnp.float32),
            pltpu.VMEM((depth, cols), jnp.float32),
            pltpu.SemaphoreType.DMA((2, count)),
        ],
        compiler_params=pltpu.CompilerParams(vmem_limit_bytes=40 * MIB),
        name="ladder",
    )(mask, side, amplitudes, integrals)


def finish_kernel(mirror_ref, own_ref, other_ref, out_ref):
    rows = own_ref.shape[1]
    lanes = 128
    for j in range(0, rows, lanes):
        index = jnp.broadcast_to(mirror_ref[:, j:j + lanes], (own_ref.shape[0], lanes))
        local = index % lanes
        picked = jnp.zeros(index.shape, jnp.float32)
        for k in range(0, rows, lanes):
            found = jnp.take_along_axis(other_ref[:, k:k + lanes], local, axis=1)
            picked = jnp.where(index // lanes == k // lanes, found, picked)
        out_ref[:, j:j + lanes] = own_ref[:, j:j + lanes] + picked


def finish(mirror, own, other):
    return pl.pallas_call(
        finish_kernel,
        out_shape=jax.ShapeDtypeStruct(own.shape, own.dtype),
        in_specs=[pl.BlockSpec(memory_space=pltpu.VMEM)] * 3,
        out_specs=pl.BlockSpec(memory_space=pltpu.VMEM),
        name="finish",
    )(mirror, own, other)


def shards(amplitudes, integrals, tile_mask, mirror_row):
    n, g = lax.axis_size("virt"), lax.axis_size("pair")
    v = lax.axis_index("virt")
    side, chip = v % 2, v // 2
    half = n // 2
    both = ladder(n, tile_mask.T, side.reshape(1), amplitudes, integrals)
    arrived = lax.ppermute(both[1], "virt", [(i, i ^ 1) for i in range(n)])
    mine = both[0] + arrived
    reduced = lax.dynamic_index_in_dim(mine, chip, 0, keepdims=False)
    came = []
    for s in range(1, half):
        block = lax.dynamic_index_in_dim(mine, (chip + s) % half, 0, keepdims=False)
        came.append(lax.ppermute(block, "virt", [(i, (i + 2 * s) % n) for i in range(n)]))
    for block in came:
        reduced = reduced + block
    route = [(i * g + q, ((i + half) % n) * g + (q + g // 2) % g) for i in range(n) for q in range(g)]
    turned = lax.ppermute(reduced, ("virt", "pair"), route)
    return finish(mirror_row.reshape(1, -1), reduced, turned).T


def solution(mesh):
    in_specs = (P("pair", "virt"), P("virt", None), P("virt", None), P("pair"))
    out_specs = P("pair", "virt")
    return jax.shard_map(shards, mesh=mesh, in_specs=in_specs, out_specs=out_specs, check_vma=False)
```

```python
import functools

import jax
import jax.numpy as jnp
from jax import lax
from jax.experimental import pallas as pl
from jax.experimental.pallas import tpu as pltpu
from jax.sharding import PartitionSpec as P

CHUNK = 512
MIB = 1 << 20


def split(x):
    high = x.astype(jnp.bfloat16)
    low = (x - high.astype(jnp.float32)).astype(jnp.bfloat16)
    return high, low


def chunks_of(extent):
    return [(start, min(CHUNK, extent - start)) for start in range(0, extent, CHUNK)]


def ladder_kernel(parts, side_ref, mask_hbm, mirror_hbm, amp_ref, int_ref, out_ref, mirror_out, mask_ref, amp, ints, sems, sem2):
    depth, cols = int_ref.shape
    rows = amp_ref.shape[0]
    spans = chunks_of(depth)
    small = [pltpu.make_async_copy(mask_hbm, mask_ref, sem2.at[0]), pltpu.make_async_copy(mirror_hbm, mirror_out, sem2.at[1])]
    for copy in small:
        copy.start()
    copies = []
    for i, (start, size) in enumerate(spans):
        span = pl.ds(start, size)
        one = pltpu.make_async_copy(amp_ref.at[:, span], amp.at[:, span], sems.at[0, i])
        two = pltpu.make_async_copy(int_ref.at[span, :], ints.at[span, :], sems.at[1, i])
        one.start()
        two.start()
        copies.append((one, two))

    col_tiles, tile_rows = mask_ref.shape
    tile_r, tile_c = depth // tile_rows, cols // col_tiles
    lane = lax.broadcasted_iota(jnp.int32, (1, cols), 1)
    total = jnp.zeros((rows, cols), jnp.float32)
    for copy in small:
        copy.wait()
    for (start, size), (one, two) in zip(spans, copies):
        one.wait()
        two.wait()
        pieces = []
        at = start
        while at < start + size:
            t = at // tile_r
            end = min((t + 1) * tile_r, start + size)
            factor = jnp.full((1, cols), mask_ref[0, t].astype(jnp.float32))
            for u in range(1, col_tiles):
                factor = jnp.where(lane >= u * tile_c, mask_ref[u, t].astype(jnp.float32), factor)
            pieces.append(ints[at:end, :] * factor)
            at = end
        masked = jnp.concatenate(pieces, axis=0)
        b_high, b_low = split(masked)
        a_high, a_low = split(amp[:, start:start + size])
        dot = functools.partial(jnp.dot, preferred_element_type=jnp.float32)
        total += dot(a_high, b_high) + dot(a_high, b_low) + dot(a_low, b_high)
    turned = total.T
    block = cols // parts
    for b in range(parts):
        out_ref[(b % 2) ^ side_ref[0], b // 2] = turned[b * block:(b + 1) * block, :]


def ladder(parts, side, mask, mirror, amplitudes, integrals):
    rows, depth = amplitudes.shape
    cols = integrals.shape[1]
    count = len(chunks_of(depth))
    return pl.pallas_call(
        functools.partial(ladder_kernel, parts),
        out_shape=(
            jax.ShapeDtypeStruct((2, parts // 2, cols // parts, rows), jnp.float32),
            jax.ShapeDtypeStruct(mirror.shape, mirror.dtype),
        ),
        in_specs=[pl.BlockSpec(memory_space=pltpu.SMEM)] + [pl.BlockSpec(memory_space=pltpu.HBM)] * 4,
        out_specs=(pl.BlockSpec(memory_space=pltpu.VMEM),) * 2,
        scratch_shapes=[
            pltpu.SMEM(mask.shape, mask.dtype),
            pltpu.VMEM((rows, depth), jnp.float32),
            pltpu.VMEM((depth, cols), jnp.float32),
            pltpu.SemaphoreType.DMA((2, count)),
            pltpu.SemaphoreType.DMA((2,)),
        ],
        compiler_params=pltpu.CompilerParams(vmem_limit_bytes=16 * MIB),
        name="ladder",
    )(side, *(pltpu.with_memory_space_constraint(x, pltpu.HBM) for x in (mask, mirror, amplitudes, integrals)))


def finish_kernel(mirror_ref, own_ref, other_ref, out_ref):
    rows = own_ref.shape[1]
    lanes = 128
    for j in range(0, rows, lanes):
        index = jnp.broadcast_to(mirror_ref[:, j:j + lanes], (own_ref.shape[0], lanes))
        local = index % lanes
        picked = jnp.zeros(index.shape, jnp.float32)
        for k in range(0, rows, lanes):
            found = jnp.take_along_axis(other_ref[:, k:k + lanes], local, axis=1)
            picked = jnp.where(index // lanes == k // lanes, found, picked)
        out_ref[:, j:j + lanes] = own_ref[:, j:j + lanes] + picked


def finish(mirror, own, other):
    return pl.pallas_call(
        finish_kernel,
        out_shape=jax.ShapeDtypeStruct(own.shape, own.dtype),
        in_specs=[pl.BlockSpec(memory_space=pltpu.VMEM)] * 3,
        out_specs=pl.BlockSpec(memory_space=pltpu.VMEM),
        compiler_params=pltpu.CompilerParams(vmem_limit_bytes=4 * MIB),
        name="finish",
    )(mirror, own, other)


def shards(amplitudes, integrals, tile_mask, mirror_row):
    n, g = lax.axis_size("virt"), lax.axis_size("pair")
    v = lax.axis_index("virt")
    side, chip = v % 2, v // 2
    half = n // 2
    both, mirror = ladder(n, side.reshape(1), tile_mask.T, mirror_row.reshape(1, -1), amplitudes, integrals)
    arrived = lax.ppermute(both[1], "virt", [(i, i ^ 1) for i in range(n)])
    mine = both[0] + arrived
    reduced = lax.dynamic_index_in_dim(mine, chip, 0, keepdims=False)
    came = []
    for s in range(1, half):
        block = lax.dynamic_index_in_dim(mine, (chip + s) % half, 0, keepdims=False)
        came.append(lax.ppermute(block, "virt", [(i, (i + 2 * s) % n) for i in range(n)]))
    for block in came:
        reduced = reduced + block
    route = [(i * g + q, ((i + half) % n) * g + (q + g // 2) % g) for i in range(n) for q in range(g)]
    turned = lax.ppermute(reduced, ("virt", "pair"), route)
    return finish(mirror, reduced, turned).T


def solution(mesh):
    in_specs = (P("pair", "virt"), P("virt", None), P("virt", None), P("pair"))
    out_specs = P("pair", "virt")
    return jax.shard_map(shards, mesh=mesh, in_specs=in_specs, out_specs=out_specs, check_vma=False)
```

```python
import functools

import jax
import jax.numpy as jnp
from jax import lax
from jax.experimental import pallas as pl
from jax.experimental.pallas import tpu as pltpu
from jax.sharding import PartitionSpec as P

CHUNK = 512
MIB = 1 << 20


def split(x):
    high = x.astype(jnp.bfloat16)
    low = (x - high.astype(jnp.float32)).astype(jnp.bfloat16)
    return high, low


def chunks_of(extent):
    starts = list(range(0, max(extent - CHUNK, 1), CHUNK))
    return list(zip(starts, [b - a for a, b in zip(starts, starts[1:] + [extent])]))


def ladder_kernel(place, mask_hbm, amp_hbm, int_hbm, out_ref, mask_ref, amp, ints, sems, small_sem):
    depth, cols = int_hbm.shape
    rows = amp_hbm.shape[0]
    spans = chunks_of(depth)
    small = pltpu.make_async_copy(mask_hbm, mask_ref, small_sem)
    large = []
    for i, (start, size) in enumerate(spans):
        span = pl.ds(start, size)
        large.append((
            pltpu.make_async_copy(amp_hbm.at[:, span], amp.at[:, span], sems.at[0, i]),
            pltpu.make_async_copy(int_hbm.at[span, :], ints.at[span, :], sems.at[1, i]),
        ))
    small.start()
    for pair in large:
        for copy in pair:
            copy.start()

    col_tiles, tile_rows = mask_ref.shape
    tile_r, tile_c = depth // tile_rows, cols // col_tiles
    lane = lax.broadcasted_iota(jnp.int32, (1, cols), 1)
    total = jnp.zeros((rows, cols), jnp.float32)
    small.wait()
    dot = functools.partial(jnp.dot, preferred_element_type=jnp.float32)
    for (start, size), pair in zip(spans, large):
        for copy in pair:
            copy.wait()
        pieces = []
        at = start
        while at < start + size:
            t = at // tile_r
            end = min((t + 1) * tile_r, start + size)
            factor = jnp.full((1, cols), mask_ref[0, t].astype(jnp.float32))
            for u in range(1, col_tiles):
                factor = jnp.where(lane >= u * tile_c, mask_ref[u, t].astype(jnp.float32), factor)
            pieces.append(ints[at:end, :] * factor)
            at = end
        b_high, b_low = split(jnp.concatenate(pieces, axis=0))
        a_high, a_low = split(amp[:, start:start + size])
        wide = dot(a_high, jnp.concatenate([b_high, b_low], axis=1))
        total += wide[:, :cols] + wide[:, cols:] + dot(a_low, b_high)
    turned = total.T
    block = out_ref.shape[-2]
    for b in range(cols // block):
        where = place(b)
        out_ref[where] = turned[b * block:(b + 1) * block, :]


def ladder(parts, place, mask, amplitudes, integrals):
    rows, depth = amplitudes.shape
    cols = integrals.shape[1]
    count = len(chunks_of(depth))
    operands = [pltpu.with_memory_space_constraint(x, pltpu.HBM) for x in (mask, amplitudes, integrals)]
    return pl.pallas_call(
        functools.partial(ladder_kernel, place),
        out_shape=jax.ShapeDtypeStruct((2, parts // 2, cols // parts, rows), jnp.float32),
        in_specs=[pl.BlockSpec(memory_space=pltpu.HBM)] * 3,
        out_specs=pl.BlockSpec(memory_space=pltpu.VMEM),
        scratch_shapes=[
            pltpu.SMEM(mask.shape, mask.dtype),
            pltpu.VMEM((rows, depth), jnp.float32),
            pltpu.VMEM((depth, cols), jnp.float32),
            pltpu.SemaphoreType.DMA((2, count)),
            pltpu.SemaphoreType.DMA,
        ],
        compiler_params=pltpu.CompilerParams(vmem_limit_bytes=16 * MIB),
        name="ladder",
    )(*operands)


def finish_kernel(mirror_ref, own_ref, other_ref, out_ref):
    rows = own_ref.shape[1]
    lanes = 128
    for j in range(0, rows, lanes):
        index = jnp.broadcast_to(mirror_ref[:, j:j + lanes], (own_ref.shape[0], lanes))
        picked = own_ref[:, j:j + lanes]
        for k in range(0, rows, lanes):
            inside = (index >= k) & (index < k + lanes)
            found = jnp.take_along_axis(other_ref[:, k:k + lanes], jnp.where(inside, index - k, 0), axis=1)
            picked += jnp.where(inside, found, 0.0)
        out_ref[:, j:j + lanes] = picked


def finish(mirror, own, other):
    return pl.pallas_call(
        finish_kernel,
        out_shape=jax.ShapeDtypeStruct(own.shape, own.dtype),
        in_specs=[pl.BlockSpec(memory_space=pltpu.VMEM)] * 3,
        out_specs=pl.BlockSpec(memory_space=pltpu.VMEM),
        compiler_params=pltpu.CompilerParams(vmem_limit_bytes=4 * MIB),
        name="finish",
    )(mirror, own, other)


def shards(amplitudes, integrals, tile_mask, mirror_row):
    n, g = lax.axis_size("virt"), lax.axis_size("pair")
    chips = n // 2

    def place(b):
        v = lax.axis_index("virt")
        side, chip = lax.rem(v, 2), lax.div(v, 2)
        s = lax.rem(b // 2 - chip + chips, chips)
        sender = jnp.where(s == 0, b % 2, 1 - b % 2)
        return jnp.where(sender == side, 0, 1), s

    both = ladder(n, place, tile_mask.T, amplitudes, integrals)
    mine = both[0] + lax.ppermute(both[1], "virt", [(i, i ^ 1) for i in range(n)])
    reduced = mine[0]
    came = []
    for s in range(1, chips):
        came.append(lax.ppermute(mine[s], "virt", [(i, ((i + 2 * s) % n) ^ 1) for i in range(n)]))
    for block in came:
        reduced = reduced + block
    route = [(i * g + q, ((i + chips) % n) * g + (q + g // 2) % g) for i in range(n) for q in range(g)]
    turned = lax.ppermute(reduced, ("virt", "pair"), route)
    return finish(mirror_row.reshape(1, -1), reduced, turned).T


def solution(mesh):
    in_specs = (P("pair", "virt"), P("virt", None), P("virt", None), P("pair"))
    out_specs = P("pair", "virt")
    return jax.shard_map(shards, mesh=mesh, in_specs=in_specs, out_specs=out_specs, check_vma=False)
```

```python
import functools

import jax
import jax.numpy as jnp
from jax import lax
from jax.experimental import pallas as pl
from jax.experimental.pallas import tpu as pltpu
from jax.sharding import PartitionSpec as P

CHUNK = 512
MIB = 1 << 20


def split(x):
    high = x.astype(jnp.bfloat16)
    low = (x - high.astype(jnp.float32)).astype(jnp.bfloat16)
    return high, low


def chunks_of(extent):
    starts = list(range(0, max(extent - CHUNK, 1), CHUNK))
    return list(zip(starts, [b - a for a, b in zip(starts, starts[1:] + [extent])]))


def ladder_kernel(place, mask_hbm, amp_hbm, int_hbm, out_ref, mask_ref, amp, ints, sems, small_sem):
    depth, cols = int_hbm.shape
    rows = amp_hbm.shape[0]
    spans = chunks_of(depth)
    small = pltpu.make_async_copy(mask_hbm, mask_ref, small_sem)
    large = []
    for i, (start, size) in enumerate(spans):
        span = pl.ds(start, size)
        large.append((
            pltpu.make_async_copy(amp_hbm.at[:, span], amp.at[:, span], sems.at[0, i]),
            pltpu.make_async_copy(int_hbm.at[span, :], ints.at[span, :], sems.at[1, i]),
        ))
    small.start()
    for pair in large:
        for copy in pair:
            copy.start()

    col_tiles, tile_rows = mask_ref.shape
    tile_r, tile_c = depth // tile_rows, cols // col_tiles
    lane = lax.broadcasted_iota(jnp.int32, (1, cols), 1)
    total = jnp.zeros((rows, cols), jnp.float32)
    small.wait()
    dot = functools.partial(jnp.dot, preferred_element_type=jnp.float32)
    for (start, size), pair in zip(spans, large):
        for copy in pair:
            copy.wait()
        pieces = []
        at = start
        while at < start + size:
            t = at // tile_r
            end = min((t + 1) * tile_r, start + size)
            factor = jnp.full((1, cols), mask_ref[0, t].astype(jnp.float32))
            for u in range(1, col_tiles):
                factor = jnp.where(lane >= u * tile_c, mask_ref[u, t].astype(jnp.float32), factor)
            pieces.append(ints[at:end, :] * factor)
            at = end
        b_high, b_low = split(jnp.concatenate(pieces, axis=0))
        a_high, a_low = split(amp[:, start:start + size])
        wide = dot(a_high, jnp.concatenate([b_high, b_low], axis=1))
        total += wide[:, :cols] + wide[:, cols:] + dot(a_low, b_high)
    turned = total.T
    block = out_ref.shape[-2]
    for b in range(cols // block):
        where = place(b)
        out_ref[where] = turned[b * block:(b + 1) * block, :]


def ladder(parts, place, mask, amplitudes, integrals):
    rows, depth = amplitudes.shape
    cols = integrals.shape[1]
    count = len(chunks_of(depth))
    operands = [pltpu.with_memory_space_constraint(x, pltpu.HBM) for x in (mask, amplitudes, integrals)]
    return pl.pallas_call(
        functools.partial(ladder_kernel, place),
        out_shape=jax.ShapeDtypeStruct((parts, cols // parts, rows), jnp.float32),
        in_specs=[pl.BlockSpec(memory_space=pltpu.HBM)] * 3,
        out_specs=pl.BlockSpec(memory_space=pltpu.VMEM),
        scratch_shapes=[
            pltpu.SMEM(mask.shape, mask.dtype),
            pltpu.VMEM((rows, depth), jnp.float32),
            pltpu.VMEM((depth, cols), jnp.float32),
            pltpu.SemaphoreType.DMA((2, count)),
            pltpu.SemaphoreType.DMA,
        ],
        compiler_params=pltpu.CompilerParams(vmem_limit_bytes=16 * MIB),
        name="ladder",
    )(*operands)


def finish_kernel(mirror_ref, own_ref, other_ref, out_ref):
    rows = own_ref.shape[1]
    lanes = 128
    for j in range(0, rows, lanes):
        index = jnp.broadcast_to(mirror_ref[:, j:j + lanes], (own_ref.shape[0], lanes))
        picked = own_ref[:, j:j + lanes]
        for k in range(0, rows, lanes):
            inside = (index >= k) & (index < k + lanes)
            found = jnp.take_along_axis(other_ref[:, k:k + lanes], jnp.where(inside, index - k, 0), axis=1)
            picked += jnp.where(inside, found, 0.0)
        out_ref[:, j:j + lanes] = picked


def finish(mirror, own, other):
    return pl.pallas_call(
        finish_kernel,
        out_shape=jax.ShapeDtypeStruct(own.shape, own.dtype),
        in_specs=[pl.BlockSpec(memory_space=pltpu.VMEM)] * 3,
        out_specs=pl.BlockSpec(memory_space=pltpu.VMEM),
        compiler_params=pltpu.CompilerParams(vmem_limit_bytes=4 * MIB),
        name="finish",
    )(mirror, own, other)


def shards(amplitudes, integrals, tile_mask, mirror_row):
    n, g = lax.axis_size("virt"), lax.axis_size("pair")
    chips = n // 2
    rest = chips - 1

    def place(b):
        v = lax.axis_index("virt")
        side, chip = lax.rem(v, 2), lax.div(v, 2)
        s = (b // 2) ^ chip
        keeper = jnp.where(s == 0, b % 2, 1 - b % 2)
        spot = jnp.where(keeper == side, 0, rest) + jnp.where(s == 0, 0, s - 1)
        return jnp.where(s == 1, 2 * rest + b % 2, spot)

    def route(s):
        return [(i, i ^ (2 * s + 1)) for i in range(n)]

    swap = [(i, i ^ 1) for i in range(n)]
    blocks = ladder(n, place, tile_mask.T, amplitudes, integrals)
    arrived = lax.ppermute(blocks[rest:2 * rest], "virt", swap)
    early = lax.ppermute(blocks[2 * rest:], "virt", route(1))
    mine = blocks[:rest] + arrived
    came = [lax.ppermute(mine[s - 1], "virt", route(s)) for s in range(2, chips)]
    if came:
        early, came[0] = lax.optimization_barrier((early, came[0]))
    side = lax.axis_index("virt") % 2
    keep = lax.dynamic_index_in_dim(early, side, 0, keepdims=False)
    give = lax.dynamic_index_in_dim(early, 1 - side, 0, keepdims=False)
    reduced = mine[0] + keep + lax.ppermute(give, "virt", swap)
    for block in came:
        reduced = reduced + block
    over = [(i * g + q, (i + chips) % n * g + (q + g // 2) % g) for i in range(n) for q in range(g)]
    turned = lax.ppermute(reduced, ("virt", "pair"), over)
    return finish(mirror_row.reshape(1, -1), reduced, turned).T


def solution(mesh):
    in_specs = (P("pair", "virt"), P("virt", None), P("virt", None), P("pair"))
    out_specs = P("pair", "virt")
    return jax.shard_map(shards, mesh=mesh, in_specs=in_specs, out_specs=out_specs, check_vma=False)
```

```python
import functools

import jax
import jax.numpy as jnp
from jax import lax
from jax.experimental import pallas as pl
from jax.experimental.pallas import tpu as pltpu
from jax.sharding import PartitionSpec as P

CHUNK = 512
MIB = 1 << 20


def split(x):
    high = x.astype(jnp.bfloat16)
    low = (x - high.astype(jnp.float32)).astype(jnp.bfloat16)
    return high, low


def chunks_of(extent):
    starts = list(range(0, max(extent - CHUNK, 1), CHUNK))
    return list(zip(starts, [b - a for a, b in zip(starts, starts[1:] + [extent])]))


def ladder_kernel(place, mask_hbm, amp_hbm, int_hbm, out_ref, mask_ref, amp, ints, sems, small_sem):
    depth, cols = int_hbm.shape
    rows = amp_hbm.shape[0]
    spans = chunks_of(depth)
    small = pltpu.make_async_copy(mask_hbm, mask_ref, small_sem)
    large = []
    for i, (start, size) in enumerate(spans):
        span = pl.ds(start, size)
        large.append((
            pltpu.make_async_copy(amp_hbm.at[:, span], amp.at[:, span], sems.at[0, i]),
            pltpu.make_async_copy(int_hbm.at[span, :], ints.at[span, :], sems.at[1, i]),
        ))
    small.start()
    for pair in large:
        for copy in pair:
            copy.start()

    col_tiles, tile_rows = mask_ref.shape
    tile_r, tile_c = depth // tile_rows, cols // col_tiles
    lane = lax.broadcasted_iota(jnp.int32, (1, cols), 1)
    total = jnp.zeros((rows, cols), jnp.float32)
    small.wait()
    dot = functools.partial(jnp.dot, preferred_element_type=jnp.float32)
    for (start, size), pair in zip(spans, large):
        for copy in pair:
            copy.wait()
        pieces = []
        at = start
        while at < start + size:
            t = at // tile_r
            end = min((t + 1) * tile_r, start + size)
            factor = jnp.full((1, cols), mask_ref[0, t].astype(jnp.float32))
            for u in range(1, col_tiles):
                factor = jnp.where(lane >= u * tile_c, mask_ref[u, t].astype(jnp.float32), factor)
            pieces.append(ints[at:end, :] * factor)
            at = end
        b_high, b_low = split(jnp.concatenate(pieces, axis=0))
        a_high, a_low = split(amp[:, start:start + size])
        wide = dot(a_high, jnp.concatenate([b_high, b_low], axis=1))
        total += wide[:, :cols] + wide[:, cols:] + dot(a_low, b_high)
    turned = total.T
    block = out_ref.shape[-2]
    for b in range(cols // block):
        where = place(b)
        out_ref[where] = turned[b * block:(b + 1) * block, :]


def ladder(parts, place, mask, amplitudes, integrals):
    rows, depth = amplitudes.shape
    cols = integrals.shape[1]
    count = len(chunks_of(depth))
    operands = [pltpu.with_memory_space_constraint(x, pltpu.HBM) for x in (mask, amplitudes, integrals)]
    return pl.pallas_call(
        functools.partial(ladder_kernel, place),
        out_shape=jax.ShapeDtypeStruct((parts, cols // parts, rows), jnp.float32),
        in_specs=[pl.BlockSpec(memory_space=pltpu.HBM)] * 3,
        out_specs=pl.BlockSpec(memory_space=pltpu.VMEM),
        scratch_shapes=[
            pltpu.SMEM(mask.shape, mask.dtype),
            pltpu.VMEM((rows, depth), jnp.float32),
            pltpu.VMEM((depth, cols), jnp.float32),
            pltpu.SemaphoreType.DMA((2, count)),
            pltpu.SemaphoreType.DMA,
        ],
        compiler_params=pltpu.CompilerParams(vmem_limit_bytes=16 * MIB),
        name="ladder",
    )(*operands)


def finish_kernel(mirror_ref, other_ref, own_ref, out_ref):
    rows = own_ref.shape[1]
    lanes = 128
    for j in range(0, rows, lanes):
        index = jnp.broadcast_to(mirror_ref[:, j:j + lanes], (own_ref.shape[0], lanes))
        picked = own_ref[:, j:j + lanes]
        for k in range(0, rows, lanes):
            inside = (index >= k) & (index < k + lanes)
            found = jnp.take_along_axis(other_ref[:, k:k + lanes], jnp.where(inside, index - k, 0), axis=1)
            picked += jnp.where(inside, found, 0.0)
        out_ref[:, j:j + lanes] = picked


def finish(mirror, other, own):
    return pl.pallas_call(
        finish_kernel,
        out_shape=jax.ShapeDtypeStruct(own.shape, own.dtype),
        in_specs=[pl.BlockSpec(memory_space=pltpu.VMEM)] * 3,
        out_specs=pl.BlockSpec(memory_space=pltpu.VMEM),
        compiler_params=pltpu.CompilerParams(vmem_limit_bytes=4 * MIB),
        name="finish",
    )(mirror, other, own)


def shards(amplitudes, integrals, tile_mask, mirror_row):
    n, g = lax.axis_size("virt"), lax.axis_size("pair")
    chips = n // 2
    rest = chips - 1
    ring = [i ^ (i >> 1) for i in range(chips)]
    if sorted(ring) != list(range(chips)):
        ring = list(range(chips))
    distances = [d for near in range(1, chips // 2 + 1) for d in (near, chips - near)][:rest]

    def place(b):
        v = lax.axis_index("virt")
        side, chip = lax.rem(v, 2), lax.div(v, 2)
        here = sum(jnp.where(chip == c, ring.index(c), 0) for c in range(chips))
        ahead = lax.rem(ring.index(b // 2) - here + chips, chips)
        step = jnp.where(2 * ahead > chips, 2 * (chips - ahead), jnp.maximum(2 * ahead - 1, 0))
        keeper = jnp.where(step == 0, 1 - b % 2, b % 2)
        spot = jnp.where(keeper == side, 0, rest) + jnp.maximum(step - 1, 0)
        return jnp.where(step == 1, 2 * rest + b % 2, spot)

    def route(step):
        ahead = distances[step - 1]
        return [(2 * ring[p] + k, 2 * ring[(p + ahead) % chips] + 1 - k) for p in range(chips) for k in range(2)]

    swap = [(i, i ^ 1) for i in range(n)]
    blocks = ladder(n, place, tile_mask.T, amplitudes, integrals)
    arrived = lax.ppermute(blocks[rest:2 * rest], "virt", swap)
    early = lax.ppermute(blocks[2 * rest:], "virt", route(1))
    mine = blocks[:rest] + arrived
    came = [lax.ppermute(mine[step - 1], "virt", route(step)) for step in range(2, chips)]
    if came:
        early, came[0] = lax.optimization_barrier((early, came[0]))
    side = lax.axis_index("virt") % 2
    keep = lax.dynamic_index_in_dim(early, 1 - side, 0, keepdims=False)
    give = lax.dynamic_index_in_dim(early, side, 0, keepdims=False)
    reduced = mine[0] + keep + lax.ppermute(give, "virt", swap)
    for block in came:
        reduced = reduced + block
    over = [(i * g + q, ((i + chips) % n ^ 1) * g + (q + g // 2) % g) for i in range(n) for q in range(g)]
    turned = lax.ppermute(reduced, ("virt", "pair"), over)
    own = lax.ppermute(reduced, "virt", swap)
    return finish(mirror_row.reshape(1, -1), turned, own).T


def solution(mesh):
    in_specs = (P("pair", "virt"), P("virt", None), P("virt", None), P("pair"))
    out_specs = P("pair", "virt")
    return jax.shard_map(shards, mesh=mesh, in_specs=in_specs, out_specs=out_specs, check_vma=False)
```

```python
import functools

import jax
import jax.numpy as jnp
from jax import lax
from jax.experimental import pallas as pl
from jax.experimental.pallas import tpu as pltpu
from jax.sharding import PartitionSpec as P

CHUNK = 512
MIB = 1 << 20


def split(x):
    high = x.astype(jnp.bfloat16)
    low = (x - high.astype(jnp.float32)).astype(jnp.bfloat16)
    return high, low


def chunks_of(extent):
    starts = list(range(0, max(extent - CHUNK, 1), CHUNK))
    return list(zip(starts, [b - a for a, b in zip(starts, starts[1:] + [extent])]))


def ladder_kernel(place, mask_hbm, amp_hbm, int_hbm, out_ref, mask_ref, amp, ints, sems, small_sem):
    depth, cols = int_hbm.shape
    rows = amp_hbm.shape[0]
    spans = chunks_of(depth)
    small = pltpu.make_async_copy(mask_hbm, mask_ref, small_sem)
    large = []
    for i, (start, size) in enumerate(spans):
        span = pl.ds(start, size)
        large.append((
            pltpu.make_async_copy(amp_hbm.at[:, span], amp.at[:, span], sems.at[0, i]),
            pltpu.make_async_copy(int_hbm.at[span, :], ints.at[span, :], sems.at[1, i]),
        ))
    small.start()
    for pair in large:
        for copy in pair:
            copy.start()

    col_tiles, tile_rows = mask_ref.shape
    tile_r, tile_c = depth // tile_rows, cols // col_tiles
    lane = lax.broadcasted_iota(jnp.int32, (1, cols), 1)
    total = jnp.zeros((rows, cols), jnp.float32)
    small.wait()
    dot = functools.partial(jnp.dot, preferred_element_type=jnp.float32)
    for (start, size), pair in zip(spans, large):
        for copy in pair:
            copy.wait()
        pieces = []
        at = start
        while at < start + size:
            t = at // tile_r
            end = min((t + 1) * tile_r, start + size)
            factor = jnp.full((1, cols), mask_ref[0, t].astype(jnp.float32))
            for u in range(1, col_tiles):
                factor = jnp.where(lane >= u * tile_c, mask_ref[u, t].astype(jnp.float32), factor)
            pieces.append(ints[at:end, :] * factor)
            at = end
        b_high, b_low = split(jnp.concatenate(pieces, axis=0))
        a_high, a_low = split(amp[:, start:start + size])
        wide = dot(a_high, jnp.concatenate([b_high, b_low], axis=1))
        total += wide[:, :cols] + wide[:, cols:] + dot(a_low, b_high)
    turned = total.T
    block = out_ref.shape[-2]
    for b in range(cols // block):
        where = place(b)
        out_ref[where] = turned[b * block:(b + 1) * block, :]


def ladder(parts, place, mask, amplitudes, integrals):
    rows, depth = amplitudes.shape
    cols = integrals.shape[1]
    count = len(chunks_of(depth))
    operands = [pltpu.with_memory_space_constraint(x, pltpu.HBM) for x in (mask, amplitudes, integrals)]
    return pl.pallas_call(
        functools.partial(ladder_kernel, place),
        out_shape=jax.ShapeDtypeStruct((parts, cols // parts, rows), jnp.float32),
        in_specs=[pl.BlockSpec(memory_space=pltpu.HBM)] * 3,
        out_specs=pl.BlockSpec(memory_space=pltpu.VMEM),
        scratch_shapes=[
            pltpu.SMEM(mask.shape, mask.dtype),
            pltpu.VMEM((rows, depth), jnp.float32),
            pltpu.VMEM((depth, cols), jnp.float32),
            pltpu.SemaphoreType.DMA((2, count)),
            pltpu.SemaphoreType.DMA,
        ],
        compiler_params=pltpu.CompilerParams(vmem_limit_bytes=16 * MIB),
        name="ladder",
    )(*operands)


def finish_kernel(mirror_ref, other_ref, own_ref, out_ref):
    rows = own_ref.shape[1]
    lanes = 128
    for j in range(0, rows, lanes):
        index = jnp.broadcast_to(mirror_ref[:, j:j + lanes], (own_ref.shape[0], lanes))
        picked = own_ref[:, j:j + lanes]
        for k in range(0, rows, lanes):
            inside = (index >= k) & (index < k + lanes)
            found = jnp.take_along_axis(other_ref[:, k:k + lanes], jnp.where(inside, index - k, 0), axis=1)
            picked += jnp.where(inside, found, 0.0)
        out_ref[:, j:j + lanes] = picked


def finish(mirror, other, own):
    return pl.pallas_call(
        finish_kernel,
        out_shape=jax.ShapeDtypeStruct(own.shape, own.dtype),
        in_specs=[pl.BlockSpec(memory_space=pltpu.VMEM)] * 3,
        out_specs=pl.BlockSpec(memory_space=pltpu.VMEM),
        compiler_params=pltpu.CompilerParams(vmem_limit_bytes=4 * MIB),
        name="finish",
    )(mirror, other, own)


def shards(amplitudes, integrals, tile_mask, mirror_row):
    n, g = lax.axis_size("virt"), lax.axis_size("pair")
    chips = n // 2
    rest = chips - 1
    ring = [i ^ (i >> 1) for i in range(chips)]
    if sorted(ring) != list(range(chips)):
        ring = list(range(chips))
    distances = [d for near in range(1, chips // 2 + 1) for d in (near, chips - near)][:rest]

    def place(b):
        v = lax.axis_index("virt")
        side, chip = lax.rem(v, 2), lax.div(v, 2)
        here = sum(jnp.where(chip == c, ring.index(c), 0) for c in range(chips))
        opposite = ring.index((b // 2 + chips // 2) % chips)
        there = jnp.where(lax.axis_index("pair") > 0, opposite, ring.index(b // 2))
        ahead = lax.rem(there - here + chips, chips)
        step = jnp.where(2 * ahead > chips, 2 * (chips - ahead), jnp.maximum(2 * ahead - 1, 0))
        keeper = jnp.where(step == 0, 1 - b % 2, b % 2)
        spot = jnp.where(keeper == side, 0, rest) + jnp.maximum(step - 1, 0)
        return jnp.where(step == 1, 2 * rest + b % 2, spot)

    def route(step):
        ahead = distances[step - 1]
        return [(2 * ring[p] + k, 2 * ring[(p + ahead) % chips] + 1 - k) for p in range(chips) for k in range(2)]

    swap = [(i, i ^ 1) for i in range(n)]
    blocks = ladder(n, place, tile_mask.T, amplitudes, integrals)
    arrived = lax.ppermute(blocks[rest:2 * rest], "virt", swap)
    early = lax.ppermute(blocks[2 * rest:], "virt", route(1))
    mine = blocks[:rest] + arrived
    came = [lax.ppermute(mine[step - 1], "virt", route(step)) for step in range(2, chips)]
    if came:
        early, came[0] = lax.optimization_barrier((early, came[0]))
    side = lax.axis_index("virt") % 2
    keep = lax.dynamic_index_in_dim(early, 1 - side, 0, keepdims=False)
    give = lax.dynamic_index_in_dim(early, side, 0, keepdims=False)
    reduced = mine[0] + keep + lax.ppermute(give, "virt", swap)
    for block in came:
        reduced = reduced + block
    def owner(i, q):
        return (i + (chips if q > 0 else 0)) % n ^ 1

    across = [(i * g + q, (owner(i, q) + chips) % n * g + (q + g // 2) % g) for i in range(n) for q in range(g)]
    home = [(i * g + q, owner(i, q) * g + q) for i in range(n) for q in range(g)]
    turned = lax.ppermute(reduced, ("virt", "pair"), across)
    own = lax.ppermute(reduced, ("virt", "pair"), home)
    return finish(mirror_row.reshape(1, -1), turned, own).T


def solution(mesh):
    in_specs = (P("pair", "virt"), P("virt", None), P("virt", None), P("pair"))
    out_specs = P("pair", "virt")
    return jax.shard_map(shards, mesh=mesh, in_specs=in_specs, out_specs=out_specs, check_vma=False)
```

```python
import functools

import jax
import jax.numpy as jnp
from jax import lax
from jax.experimental import pallas as pl
from jax.experimental.pallas import tpu as pltpu
from jax.sharding import PartitionSpec as P

CHUNK = 512
DEPTH = 256
MIB = 1 << 20


def split(x):
    high = x.astype(jnp.bfloat16)
    low = (x - high.astype(jnp.float32)).astype(jnp.bfloat16)
    return high, low


def chunks_of(extent):
    starts = list(range(0, max(extent - CHUNK, 1), CHUNK))
    return list(zip(starts, [b - a for a, b in zip(starts, starts[1:] + [extent])]))


def ladder_kernel(place, mask_hbm, amp_hbm, int_hbm, out_ref, mask_ref, amp, ints, sems, small_sem):
    depth, cols = int_hbm.shape
    rows = amp_hbm.shape[0]
    spans = chunks_of(depth)
    small = pltpu.make_async_copy(mask_hbm, mask_ref, small_sem)
    large = []
    for i, (start, size) in enumerate(spans):
        span = pl.ds(start, size)
        large.append((
            pltpu.make_async_copy(amp_hbm.at[:, span], amp.at[:, span], sems.at[0, i]),
            pltpu.make_async_copy(int_hbm.at[span, :], ints.at[span, :], sems.at[1, i]),
        ))
    small.start()
    for pair in large:
        for copy in pair:
            copy.start()

    col_tiles, tile_rows = mask_ref.shape
    tile_r, tile_c = depth // tile_rows, cols // col_tiles
    lane = lax.broadcasted_iota(jnp.int32, (1, cols), 1)
    total = jnp.zeros((rows, cols), jnp.float32)
    small.wait()
    dot = functools.partial(jnp.dot, preferred_element_type=jnp.float32)
    for (start, size), pair in zip(spans, large):
        for copy in pair:
            copy.wait()
        pieces = []
        at = start
        while at < start + size:
            t = at // tile_r
            end = min((t + 1) * tile_r, start + size)
            factor = jnp.full((1, cols), mask_ref[0, t].astype(jnp.float32))
            for u in range(1, col_tiles):
                factor = jnp.where(lane >= u * tile_c, mask_ref[u, t].astype(jnp.float32), factor)
            pieces.append(ints[at:end, :] * factor)
            at = end
        b_high, b_low = split(jnp.concatenate(pieces, axis=0))
        a_high, a_low = split(amp[:, start:start + size])
        b_both = jnp.concatenate([b_high, b_low], axis=1)
        full = size - size % DEPTH
        spare = size - full
        if full and 2 * spare == DEPTH:
            b_spare = jnp.concatenate([b_high[full:], jnp.zeros_like(b_low[full:])], axis=1)
            wide = dot(jnp.concatenate([a_high, a_low[:, full:]], axis=1), jnp.concatenate([b_both, b_spare], axis=0))
            low = dot(a_low[:, :full], b_high[:full])
        else:
            wide = dot(a_high, b_both)
            low = dot(a_low, b_high)
        total += wide[:, :cols] + wide[:, cols:] + low
    turned = total.T
    block = out_ref.shape[-2]
    for b in range(cols // block):
        where = place(b)
        out_ref[where] = turned[b * block:(b + 1) * block, :]


def ladder(parts, place, mask, amplitudes, integrals):
    rows, depth = amplitudes.shape
    cols = integrals.shape[1]
    count = len(chunks_of(depth))
    operands = [pltpu.with_memory_space_constraint(x, pltpu.HBM) for x in (mask, amplitudes, integrals)]
    return pl.pallas_call(
        functools.partial(ladder_kernel, place),
        out_shape=jax.ShapeDtypeStruct((parts, cols // parts, rows), jnp.float32),
        in_specs=[pl.BlockSpec(memory_space=pltpu.HBM)] * 3,
        out_specs=pl.BlockSpec(memory_space=pltpu.VMEM),
        scratch_shapes=[
            pltpu.SMEM(mask.shape, mask.dtype),
            pltpu.VMEM((rows, depth), jnp.float32),
            pltpu.VMEM((depth, cols), jnp.float32),
            pltpu.SemaphoreType.DMA((2, count)),
            pltpu.SemaphoreType.DMA,
        ],
        compiler_params=pltpu.CompilerParams(vmem_limit_bytes=16 * MIB),
        name="ladder",
    )(*operands)


def finish_kernel(mirror_ref, other_ref, own_ref, out_ref):
    rows = own_ref.shape[1]
    lanes = 128
    for j in range(0, rows, lanes):
        index = jnp.broadcast_to(mirror_ref[:, j:j + lanes], (own_ref.shape[0], lanes))
        picked = own_ref[:, j:j + lanes]
        for k in range(0, rows, lanes):
            inside = (index >= k) & (index < k + lanes)
            found = jnp.take_along_axis(other_ref[:, k:k + lanes], jnp.where(inside, index - k, 0), axis=1)
            picked += jnp.where(inside, found, 0.0)
        out_ref[:, j:j + lanes] = picked


def finish(mirror, other, own):
    return pl.pallas_call(
        finish_kernel,
        out_shape=jax.ShapeDtypeStruct(own.shape, own.dtype),
        in_specs=[pl.BlockSpec(memory_space=pltpu.VMEM)] * 3,
        out_specs=pl.BlockSpec(memory_space=pltpu.VMEM),
        compiler_params=pltpu.CompilerParams(vmem_limit_bytes=4 * MIB),
        name="finish",
    )(mirror, other, own)


def shards(amplitudes, integrals, tile_mask, mirror_row):
    n, g = lax.axis_size("virt"), lax.axis_size("pair")
    chips = n // 2
    rest = chips - 1
    ring = [i ^ (i >> 1) for i in range(chips)]
    if sorted(ring) != list(range(chips)):
        ring = list(range(chips))
    distances = [d for near in range(1, chips // 2 + 1) for d in (near, chips - near)][:rest]

    def place(b):
        v = lax.axis_index("virt")
        side, chip = lax.rem(v, 2), lax.div(v, 2)
        here = sum(jnp.where(chip == c, ring.index(c), 0) for c in range(chips))
        opposite = ring.index((b // 2 + chips // 2) % chips)
        there = jnp.where(lax.axis_index("pair") > 0, opposite, ring.index(b // 2))
        ahead = lax.rem(there - here + chips, chips)
        step = jnp.where(2 * ahead > chips, 2 * (chips - ahead), jnp.maximum(2 * ahead - 1, 0))
        keeper = jnp.where(step == 0, 1 - b % 2, b % 2)
        spot = jnp.where(keeper == side, 0, rest) + jnp.maximum(step - 1, 0)
        return jnp.where(step == 1, 2 * rest + b % 2, spot)

    def route(step):
        ahead = distances[step - 1]
        return [(2 * ring[p] + k, 2 * ring[(p + ahead) % chips] + 1 - k) for p in range(chips) for k in range(2)]

    swap = [(i, i ^ 1) for i in range(n)]
    blocks = ladder(n, place, tile_mask.T, amplitudes, integrals)
    arrived = lax.ppermute(blocks[rest:2 * rest], "virt", swap)
    early = lax.ppermute(blocks[2 * rest:], "virt", route(1))
    mine = blocks[:rest] + arrived
    came = [lax.ppermute(mine[step - 1], "virt", route(step)) for step in range(2, chips)]
    if came:
        early, came[0] = lax.optimization_barrier((early, came[0]))
    side = lax.axis_index("virt") % 2
    keep = lax.dynamic_index_in_dim(early, 1 - side, 0, keepdims=False)
    give = lax.dynamic_index_in_dim(early, side, 0, keepdims=False)
    reduced = mine[0] + keep + lax.ppermute(give, "virt", swap)
    for block in came:
        reduced = reduced + block
    def owner(i, q):
        return (i + (chips if q > 0 else 0)) % n ^ 1

    across = [(i * g + q, (owner(i, q) + chips) % n * g + (q + g // 2) % g) for i in range(n) for q in range(g)]
    home = [(i * g + q, owner(i, q) * g + q) for i in range(n) for q in range(g)]
    turned = lax.ppermute(reduced, ("virt", "pair"), across)
    own = lax.ppermute(reduced, ("virt", "pair"), home)
    return finish(mirror_row.reshape(1, -1), turned, own).T


def solution(mesh):
    in_specs = (P("pair", "virt"), P("virt", None), P("virt", None), P("pair"))
    out_specs = P("pair", "virt")
    return jax.shard_map(shards, mesh=mesh, in_specs=in_specs, out_specs=out_specs, check_vma=False)
```

```python
import functools

import jax
import jax.numpy as jnp
from jax import lax
from jax.experimental import pallas as pl
from jax.experimental.pallas import tpu as pltpu
from jax.sharding import PartitionSpec as P

CHUNK = 512
DEPTH = 256
MIB = 1 << 20


def split(x):
    high = x.astype(jnp.bfloat16)
    low = (x - high.astype(jnp.float32)).astype(jnp.bfloat16)
    return high, low


def chunks_of(extent):
    starts = list(range(0, max(extent - CHUNK, 1), CHUNK))
    return list(zip(starts, [b - a for a, b in zip(starts, starts[1:] + [extent])]))


def ladder_kernel(place, mask_hbm, amp_hbm, int_hbm, out_ref, mask_ref, amp, ints, sems, small_sem):
    depth, cols = int_hbm.shape
    rows = amp_hbm.shape[0]
    spans = chunks_of(depth)
    small = pltpu.make_async_copy(mask_hbm, mask_ref, small_sem)
    large = []
    for i, (start, size) in enumerate(spans):
        span = pl.ds(start, size)
        large.append((
            pltpu.make_async_copy(amp_hbm.at[:, span], amp.at[:, span], sems.at[0, i]),
            pltpu.make_async_copy(int_hbm.at[span, :], ints.at[span, :], sems.at[1, i]),
        ))
    small.start()
    for pair in large:
        for copy in pair:
            copy.start()

    col_tiles, tile_rows = mask_ref.shape
    tile_r, tile_c = depth // tile_rows, cols // col_tiles
    lane = lax.broadcasted_iota(jnp.int32, (1, cols), 1)
    total = jnp.zeros((rows, cols), jnp.float32)
    small.wait()
    dot = functools.partial(jnp.dot, preferred_element_type=jnp.float32)
    for (start, size), pair in zip(spans, large):
        for copy in pair:
            copy.wait()
        pieces = []
        at = start
        while at < start + size:
            t = at // tile_r
            end = min((t + 1) * tile_r, start + size)
            factor = jnp.full((1, cols), mask_ref[0, t].astype(jnp.float32))
            for u in range(1, col_tiles):
                factor = jnp.where(lane >= u * tile_c, mask_ref[u, t].astype(jnp.float32), factor)
            pieces.append(ints[at:end, :] * factor)
            at = end
        b_high, b_low = split(jnp.concatenate(pieces, axis=0))
        a_high, a_low = split(amp[:, start:start + size])
        b_both = jnp.concatenate([b_high, b_low], axis=1)
        full = size - size % DEPTH
        spare = size - full
        if full and 2 * spare == DEPTH:
            b_spare = jnp.concatenate([b_high[full:], jnp.zeros_like(b_low[full:])], axis=1)
            wide = dot(jnp.concatenate([a_high, a_low[:, full:]], axis=1), jnp.concatenate([b_both, b_spare], axis=0))
            low = dot(a_low[:, :full], b_high[:full])
        else:
            wide = dot(a_high, b_both)
            low = dot(a_low, b_high)
        total += wide[:, :cols] + wide[:, cols:] + low
    turned = total.T
    block = out_ref.shape[-2]
    for b in range(cols // block):
        where = place(b)
        out_ref[where] = turned[b * block:(b + 1) * block, :]


def ladder(parts, place, mask, amplitudes, integrals):
    rows, depth = amplitudes.shape
    cols = integrals.shape[1]
    count = len(chunks_of(depth))
    operands = [pltpu.with_memory_space_constraint(x, pltpu.HBM) for x in (mask, amplitudes, integrals)]
    return pl.pallas_call(
        functools.partial(ladder_kernel, place),
        out_shape=jax.ShapeDtypeStruct((parts, cols // parts, rows), jnp.float32),
        in_specs=[pl.BlockSpec(memory_space=pltpu.HBM)] * 3,
        out_specs=pl.BlockSpec(memory_space=pltpu.VMEM),
        scratch_shapes=[
            pltpu.SMEM(mask.shape, mask.dtype),
            pltpu.VMEM((rows, depth), jnp.float32),
            pltpu.VMEM((depth, cols), jnp.float32),
            pltpu.SemaphoreType.DMA((2, count)),
            pltpu.SemaphoreType.DMA,
        ],
        compiler_params=pltpu.CompilerParams(vmem_limit_bytes=16 * MIB),
        name="ladder",
    )(*operands)


def finish_kernel(mirror_ref, other_ref, own_ref, out_ref):
    rows = own_ref.shape[1]
    lanes = 128
    for j in range(0, rows, lanes):
        index = jnp.broadcast_to(mirror_ref[:, j:j + lanes], (own_ref.shape[0], lanes))
        picked = own_ref[:, j:j + lanes]
        for k in range(0, rows, lanes):
            inside = (index >= k) & (index < k + lanes)
            found = jnp.take_along_axis(other_ref[:, k:k + lanes], jnp.where(inside, index - k, 0), axis=1)
            picked += jnp.where(inside, found, 0.0)
        out_ref[:, j:j + lanes] = picked


def finish(mirror, other, own):
    return pl.pallas_call(
        finish_kernel,
        out_shape=jax.ShapeDtypeStruct(own.shape, own.dtype),
        in_specs=[pl.BlockSpec(memory_space=pltpu.VMEM)] * 3,
        out_specs=pl.BlockSpec(memory_space=pltpu.VMEM),
        compiler_params=pltpu.CompilerParams(vmem_limit_bytes=4 * MIB),
        name="finish",
    )(mirror, other, own)


def shards(amplitudes, integrals, tile_mask, mirror_row):
    n, g = lax.axis_size("virt"), lax.axis_size("pair")
    chips = n // 2
    rest = chips - 1
    ring = [i ^ (i >> 1) for i in range(chips)]
    if sorted(ring) != list(range(chips)):
        ring = list(range(chips))
    distances = [d for near in range(1, chips // 2 + 1) for d in (near, chips - near)][:rest]

    def place(b):
        v = lax.axis_index("virt")
        side, chip = lax.rem(v, 2), lax.div(v, 2)
        here = sum(jnp.where(chip == c, ring.index(c), 0) for c in range(chips))
        opposite = ring.index((b // 2 + chips // 2) % chips)
        there = jnp.where(lax.axis_index("pair") > 0, opposite, ring.index(b // 2))
        ahead = lax.rem(there - here + chips, chips)
        step = jnp.where(2 * ahead > chips, 2 * (chips - ahead), jnp.maximum(2 * ahead - 1, 0))
        keeper = jnp.where(step == 0, 1 - b % 2, b % 2)
        spot = jnp.where(keeper == side, 0, rest) + jnp.maximum(step - 1, 0)
        return jnp.where(step == 1, 2 * rest + b % 2, spot)

    def route(step):
        ahead = distances[step - 1]
        return [(2 * ring[p] + k, 2 * ring[(p + ahead) % chips] + 1 - k) for p in range(chips) for k in range(2)]

    swap = [(i, i ^ 1) for i in range(n)]
    blocks = ladder(n, place, tile_mask.T, amplitudes, integrals)
    mine = []
    if rest > 1:
        mine = blocks[1:rest] + lax.ppermute(blocks[rest + 1:2 * rest], "virt", swap)
    early = lax.ppermute(blocks[2 * rest:], "virt", route(1))
    came = [lax.ppermute(mine[step - 2], "virt", route(step)) for step in range(2, chips)]
    if came:
        early, came[0] = lax.optimization_barrier((early, came[0]))
    side = lax.axis_index("virt") % 2
    keep = lax.dynamic_index_in_dim(early, 1 - side, 0, keepdims=False)
    give = lax.dynamic_index_in_dim(early, side, 0, keepdims=False)
    reduced = blocks[0] + keep + lax.ppermute(give + blocks[rest], "virt", swap)
    for block in came:
        reduced = reduced + block
    def owner(i, q):
        return (i + (chips if q > 0 else 0)) % n ^ 1

    across = [(i * g + q, (owner(i, q) + chips) % n * g + (q + g // 2) % g) for i in range(n) for q in range(g)]
    home = [(i * g + q, owner(i, q) * g + q) for i in range(n) for q in range(g)]
    turned = lax.ppermute(reduced, ("virt", "pair"), across)
    own = lax.ppermute(reduced, ("virt", "pair"), home)
    return finish(mirror_row.reshape(1, -1), turned, own).T


def solution(mesh):
    in_specs = (P("pair", "virt"), P("virt", None), P("virt", None), P("pair"))
    out_specs = P("pair", "virt")
    return jax.shard_map(shards, mesh=mesh, in_specs=in_specs, out_specs=out_specs, check_vma=False)
```

```python
import functools

import jax
import jax.numpy as jnp
from jax import lax
from jax.experimental import pallas as pl
from jax.experimental.pallas import tpu as pltpu
from jax.sharding import PartitionSpec as P

CHUNK = 512
DEPTH = 256
MIB = 1 << 20


def split(x):
    high = x.astype(jnp.bfloat16)
    low = (x - high.astype(jnp.float32)).astype(jnp.bfloat16)
    return high, low


def chunks_of(extent):
    starts = list(range(0, max(extent - CHUNK, 1), CHUNK))
    return list(zip(starts, [b - a for a, b in zip(starts, starts[1:] + [extent])]))


def ladder_kernel(place, mask_hbm, amp_hbm, int_hbm, out_ref, mask_ref, amp, ints, sems, small_sem):
    depth, cols = int_hbm.shape
    spans = chunks_of(depth)
    small = pltpu.make_async_copy(mask_hbm, mask_ref, small_sem)
    large = []
    for i, (start, size) in enumerate(spans):
        span = pl.ds(start, size)
        large.append((
            pltpu.make_async_copy(amp_hbm.at[:, span], amp.at[:, span], sems.at[0, i]),
            pltpu.make_async_copy(int_hbm.at[span, :], ints.at[span, :], sems.at[1, i]),
        ))
    small.start()
    for pair in large:
        for copy in pair:
            copy.start()

    col_tiles, tile_rows = mask_ref.shape
    tile_r, tile_c = depth // tile_rows, cols // col_tiles
    lane = lax.broadcasted_iota(jnp.int32, (1, cols), 1)
    total = None
    small.wait()
    dot = functools.partial(jnp.dot, preferred_element_type=jnp.float32)
    for (start, size), pair in zip(spans, large):
        for copy in pair:
            copy.wait()
        pieces = []
        at = start
        while at < start + size:
            t = at // tile_r
            end = min((t + 1) * tile_r, start + size)
            factor = jnp.full((1, cols), mask_ref[0, t].astype(jnp.float32))
            for u in range(1, col_tiles):
                factor = jnp.where(lane >= u * tile_c, mask_ref[u, t].astype(jnp.float32), factor)
            pieces.append(ints[at:end, :] * factor)
            at = end
        b_high, b_low = split(jnp.concatenate(pieces, axis=0))
        a_high, a_low = split(amp[:, start:start + size])
        b_both = jnp.concatenate([b_high, b_low], axis=1)
        full = size - size % DEPTH
        spare = size - full
        if full and 2 * spare == DEPTH:
            b_spare = jnp.concatenate([b_high[full:], jnp.zeros_like(b_low[full:])], axis=1)
            wide = dot(jnp.concatenate([a_high, a_low[:, full:]], axis=1), jnp.concatenate([b_both, b_spare], axis=0))
            low = dot(a_low[:, :full], b_high[:full])
        else:
            wide = dot(a_high, b_both)
            low = dot(a_low, b_high)
        part = wide[:, :cols] + wide[:, cols:] + low
        total = part if total is None else total + part
    turned = total.T
    block = out_ref.shape[-2]
    for b in range(cols // block):
        where = place(b)
        out_ref[where] = turned[b * block:(b + 1) * block, :]


def ladder(parts, place, mask, amplitudes, integrals):
    rows, depth = amplitudes.shape
    cols = integrals.shape[1]
    count = len(chunks_of(depth))
    operands = [pltpu.with_memory_space_constraint(x, pltpu.HBM) for x in (mask, amplitudes, integrals)]
    return pl.pallas_call(
        functools.partial(ladder_kernel, place),
        out_shape=jax.ShapeDtypeStruct((parts, cols // parts, rows), jnp.float32),
        in_specs=[pl.BlockSpec(memory_space=pltpu.HBM)] * 3,
        out_specs=pl.BlockSpec(memory_space=pltpu.VMEM),
        scratch_shapes=[
            pltpu.SMEM(mask.shape, mask.dtype),
            pltpu.VMEM((rows, depth), jnp.float32),
            pltpu.VMEM((depth, cols), jnp.float32),
            pltpu.SemaphoreType.DMA((2, count)),
            pltpu.SemaphoreType.DMA,
        ],
        compiler_params=pltpu.CompilerParams(vmem_limit_bytes=16 * MIB),
        name="ladder",
    )(*operands)


def finish_kernel(mirror_ref, other_ref, own_ref, out_ref):
    rows = own_ref.shape[1]
    lanes = 128
    for j in range(0, rows, lanes):
        index = jnp.broadcast_to(mirror_ref[:, j:j + lanes], (own_ref.shape[0], lanes))
        picked = own_ref[:, j:j + lanes]
        for k in range(0, rows, lanes):
            inside = (index >= k) & (index < k + lanes)
            found = jnp.take_along_axis(other_ref[:, k:k + lanes], jnp.where(inside, index - k, 0), axis=1)
            picked += jnp.where(inside, found, 0.0)
        out_ref[:, j:j + lanes] = picked


def finish(mirror, other, own):
    return pl.pallas_call(
        finish_kernel,
        out_shape=jax.ShapeDtypeStruct(own.shape, own.dtype),
        in_specs=[pl.BlockSpec(memory_space=pltpu.VMEM)] * 3,
        out_specs=pl.BlockSpec(memory_space=pltpu.VMEM),
        compiler_params=pltpu.CompilerParams(vmem_limit_bytes=4 * MIB),
        name="finish",
    )(mirror, other, own)


def shards(amplitudes, integrals, tile_mask, mirror_row):
    n, g = lax.axis_size("virt"), lax.axis_size("pair")
    chips = n // 2
    rest = chips - 1
    ring = [i ^ (i >> 1) for i in range(chips)]
    if sorted(ring) != list(range(chips)):
        ring = list(range(chips))
    distances = [d for near in range(1, chips // 2 + 1) for d in (near, chips - near)][:rest]

    def place(b):
        v = lax.axis_index("virt")
        side, chip = lax.rem(v, 2), lax.div(v, 2)
        here = sum(jnp.where(chip == c, ring.index(c), 0) for c in range(chips))
        opposite = ring.index((b // 2 + chips // 2) % chips)
        there = jnp.where(lax.axis_index("pair") > 0, opposite, ring.index(b // 2))
        ahead = lax.rem(there - here + chips, chips)
        step = jnp.where(2 * ahead > chips, 2 * (chips - ahead), jnp.maximum(2 * ahead - 1, 0))
        keeper = jnp.where(step == 0, 1 - b % 2, b % 2)
        spot = jnp.where(keeper == side, 0, rest) + jnp.maximum(step - 1, 0)
        return jnp.where(step == 1, 2 * rest + b % 2, spot)

    def route(step):
        ahead = distances[step - 1]
        return [(2 * ring[p] + k, 2 * ring[(p + ahead) % chips] + 1 - k) for p in range(chips) for k in range(2)]

    swap = [(i, i ^ 1) for i in range(n)]
    blocks = ladder(n, place, tile_mask.T, amplitudes, integrals)
    mine = []
    if rest > 1:
        mine = blocks[1:rest] + lax.ppermute(blocks[rest + 1:2 * rest], "virt", swap)
    early = lax.ppermute(blocks[2 * rest:], "virt", route(1))
    came = [lax.ppermute(mine[step - 2], "virt", route(step)) for step in range(2, chips)]
    if came:
        early, came[0] = lax.optimization_barrier((early, came[0]))
    side = lax.axis_index("virt") % 2
    keep = lax.dynamic_index_in_dim(early, 1 - side, 0, keepdims=False)
    give = lax.dynamic_index_in_dim(early, side, 0, keepdims=False)
    reduced = blocks[0] + keep + lax.ppermute(give + blocks[rest], "virt", swap)
    for block in came:
        reduced = reduced + block
    def owner(i, q):
        return (i + (chips if q > 0 else 0)) % n ^ 1

    across = [(i * g + q, (owner(i, q) + chips) % n * g + (q + g // 2) % g) for i in range(n) for q in range(g)]
    home = [(i * g + q, owner(i, q) * g + q) for i in range(n) for q in range(g)]
    turned = lax.ppermute(reduced, ("virt", "pair"), across)
    own = lax.ppermute(reduced, ("virt", "pair"), home)
    return finish(mirror_row.reshape(1, -1), turned, own).T


def solution(mesh):
    in_specs = (P("pair", "virt"), P("virt", None), P("virt", None), P("pair"))
    out_specs = P("pair", "virt")
    return jax.shard_map(shards, mesh=mesh, in_specs=in_specs, out_specs=out_specs, check_vma=False)
```

```python
import functools

import jax
import jax.numpy as jnp
from jax import lax
from jax.experimental import pallas as pl
from jax.experimental.pallas import tpu as pltpu
from jax.sharding import PartitionSpec as P

CHUNK = 512
DEPTH = 256
MIB = 1 << 20


def split(x):
    high = x.astype(jnp.bfloat16)
    low = (x - high.astype(jnp.float32)).astype(jnp.bfloat16)
    return high, low


def chunks_of(extent):
    starts = list(range(0, max(extent - CHUNK, 1), CHUNK))
    return list(zip(starts, [b - a for a, b in zip(starts, starts[1:] + [extent])]))


def ladder_kernel(place, mask_hbm, amp_hbm, int_hbm, out_ref, mask_ref, amp, ints, sems, small_sem):
    depth, cols = int_hbm.shape
    spans = chunks_of(depth)
    small = pltpu.make_async_copy(mask_hbm, mask_ref, small_sem)
    large = []
    for i, (start, size) in enumerate(spans):
        span = pl.ds(start, size)
        large.append((
            pltpu.make_async_copy(amp_hbm.at[:, span], amp.at[:, span], sems.at[0, i]),
            pltpu.make_async_copy(int_hbm.at[span, :], ints.at[span, :], sems.at[1, i]),
        ))
    small.start()
    for pair in large:
        for copy in pair:
            copy.start()

    col_tiles, tile_rows = mask_ref.shape
    tile_r, tile_c = depth // tile_rows, cols // col_tiles
    lane = lax.broadcasted_iota(jnp.int32, (1, cols), 1)
    total = None
    small.wait()
    dot = functools.partial(jnp.dot, preferred_element_type=jnp.float32)
    for (start, size), pair in zip(spans, large):
        for copy in pair:
            copy.wait()
        pieces = []
        at = start
        while at < start + size:
            t = at // tile_r
            end = min((t + 1) * tile_r, start + size)
            factor = jnp.full((1, cols), mask_ref[0, t].astype(jnp.float32))
            for u in range(1, col_tiles):
                factor = jnp.where(lane >= u * tile_c, mask_ref[u, t].astype(jnp.float32), factor)
            pieces.append(ints[at:end, :] * factor)
            at = end
        b_high, b_low = split(jnp.concatenate(pieces, axis=0))
        a_high, a_low = split(amp[:, start:start + size])
        b_both = jnp.concatenate([b_high, b_low], axis=1)
        full = size - size % DEPTH
        spare = size - full
        if full and 2 * spare == DEPTH:
            b_spare = jnp.concatenate([b_high[full:], jnp.zeros_like(b_low[full:])], axis=1)
            wide = dot(jnp.concatenate([a_high, a_low[:, full:]], axis=1), jnp.concatenate([b_both, b_spare], axis=0))
            low = dot(a_low[:, :full], b_high[:full])
        else:
            wide = dot(a_high, b_both)
            low = dot(a_low, b_high)
        part = wide[:, :cols] + wide[:, cols:] + low
        total = part if total is None else total + part
    turned = total.T
    block = out_ref.shape[-2]
    for b in range(cols // block):
        where = place(b)
        out_ref[where] = turned[b * block:(b + 1) * block, :]


def ladder(parts, place, mask, amplitudes, integrals):
    rows, depth = amplitudes.shape
    cols = integrals.shape[1]
    count = len(chunks_of(depth))
    operands = [pltpu.with_memory_space_constraint(x, pltpu.HBM) for x in (mask, amplitudes, integrals)]
    return pl.pallas_call(
        functools.partial(ladder_kernel, place),
        out_shape=jax.ShapeDtypeStruct((parts, cols // parts, rows), jnp.float32),
        in_specs=[pl.BlockSpec(memory_space=pltpu.HBM)] * 3,
        out_specs=pl.BlockSpec(memory_space=pltpu.VMEM),
        scratch_shapes=[
            pltpu.SMEM(mask.shape, mask.dtype),
            pltpu.VMEM((rows, depth), jnp.float32),
            pltpu.VMEM((depth, cols), jnp.float32),
            pltpu.SemaphoreType.DMA((2, count)),
            pltpu.SemaphoreType.DMA,
        ],
        compiler_params=pltpu.CompilerParams(vmem_limit_bytes=16 * MIB),
        name="ladder",
    )(*operands)


def finish_kernel(mirror_ref, other_ref, own_ref, out_ref):
    rows = own_ref.shape[1]
    lanes = 128
    for j in range(0, rows, lanes):
        index = jnp.broadcast_to(mirror_ref[:, j:j + lanes], (own_ref.shape[0], lanes))
        picked = own_ref[:, j:j + lanes]
        for k in range(0, rows, lanes):
            inside = (index >= k) & (index < k + lanes)
            found = jnp.take_along_axis(other_ref[:, k:k + lanes], jnp.where(inside, index - k, 0), axis=1)
            picked += jnp.where(inside, found, 0.0)
        out_ref[:, j:j + lanes] = picked


def finish(mirror, other, own):
    return pl.pallas_call(
        finish_kernel,
        out_shape=jax.ShapeDtypeStruct(own.shape, own.dtype),
        in_specs=[pl.BlockSpec(memory_space=pltpu.VMEM)] * 3,
        out_specs=pl.BlockSpec(memory_space=pltpu.VMEM),
        compiler_params=pltpu.CompilerParams(vmem_limit_bytes=4 * MIB),
        name="finish",
    )(mirror, other, own)


def shards(amplitudes, integrals, tile_mask, mirror_row):
    n, g = lax.axis_size("virt"), lax.axis_size("pair")
    chips = n // 2
    rest = chips - 1
    ring = [i ^ (i >> 1) for i in (-p % chips for p in range(chips))]
    if sorted(ring) != list(range(chips)):
        ring = list(range(chips))
    distances = [d for near in range(1, chips // 2 + 1) for d in (near, chips - near)][:rest]

    def place(b):
        v = lax.axis_index("virt")
        side, chip = lax.rem(v, 2), lax.div(v, 2)
        here = sum(jnp.where(chip == c, ring.index(c), 0) for c in range(chips))
        opposite = ring.index((b // 2 + chips // 2) % chips)
        there = jnp.where(lax.axis_index("pair") > 0, opposite, ring.index(b // 2))
        ahead = lax.rem(there - here + chips, chips)
        step = jnp.where(2 * ahead > chips, 2 * (chips - ahead), jnp.maximum(2 * ahead - 1, 0))
        keeper = jnp.where(step == 0, 1 - b % 2, b % 2)
        spot = jnp.where(keeper == side, 0, rest) + jnp.maximum(step - 1, 0)
        return jnp.where(step == 1, 2 * rest + b % 2, spot)

    def route(step):
        ahead = distances[step - 1]
        return [(2 * ring[p] + k, 2 * ring[(p + ahead) % chips] + 1 - k) for p in range(chips) for k in range(2)]

    swap = [(i, i ^ 1) for i in range(n)]
    blocks = ladder(n, place, tile_mask.T, amplitudes, integrals)
    mine = []
    if rest > 1:
        mine = blocks[1:rest] + lax.ppermute(blocks[rest + 1:2 * rest], "virt", swap)
    early = lax.ppermute(blocks[2 * rest:], "virt", route(1))
    came = [lax.ppermute(mine[step - 2], "virt", route(step)) for step in range(2, chips)]
    if came:
        early, came[0] = lax.optimization_barrier((early, came[0]))
    side = lax.axis_index("virt") % 2
    keep = lax.dynamic_index_in_dim(early, 1 - side, 0, keepdims=False)
    give = lax.dynamic_index_in_dim(early, side, 0, keepdims=False)
    reduced = blocks[0] + keep + lax.ppermute(give + blocks[rest], "virt", swap)
    for block in came:
        reduced = reduced + block
    def owner(i, q):
        return (i + (chips if q > 0 else 0)) % n ^ 1

    across = [(i * g + q, (owner(i, q) + chips) % n * g + (q + g // 2) % g) for i in range(n) for q in range(g)]
    home = [(i * g + q, owner(i, q) * g + q) for i in range(n) for q in range(g)]
    turned = lax.ppermute(reduced, ("virt", "pair"), across)
    own = lax.ppermute(reduced, ("virt", "pair"), home)
    return finish(mirror_row.reshape(1, -1), turned, own).T


def solution(mesh):
    in_specs = (P("pair", "virt"), P("virt", None), P("virt", None), P("pair"))
    out_specs = P("pair", "virt")
    return jax.shard_map(shards, mesh=mesh, in_specs=in_specs, out_specs=out_specs, check_vma=False)
```
